512 devices in a mesh: row: 16 (over y_lo, x, core), col: 32 (over y_hi, z).
Axes of the slice: x: 4, y: 8 (y_hi: 4, y_lo: 2; y = y_hi * 2 + y_lo), z: 8, core: 2. Of those that a mesh axis runs over, the one named last changes fastest.
Arguments:
- inputs: bfloat16 [512, 12288], P('col', 'row'), may hold values from -6 to 6
- w_in: bfloat16 [12288, 24576], P('row', 'col'), may hold values from -0.0546875 to 0.0546875
- w_out: bfloat16 [24576, 12288], P('col', 'row'), may hold values from -0.0390625 to 0.0390625
- out_grad: bfloat16 [512, 12288], P('col', 'row'), may hold values from -6 to 6
Outputs:
- grad_inputs: bfloat16 [512, 12288], P('col', 'row')
- grad_w_in: bfloat16 [12288, 24576], P('row', 'col')
- grad_w_out: bfloat16 [24576, 12288], P('col', 'row')
The draws below stay inside these ranges and needn't reach their ends.
All inputs are finite; a program needn't handle non-finite values.
Results may differ from the reference program's by a relative error of at most 0.005.
Values may be sent and summed in bfloat16 or wider, within the bound.
A program may use at most 64 MiB of HBM per device.

```python
import math
import jax
import jax.numpy as jnp
from jax import lax

D = 12288
FF = 24576
TOKENS = 512


def block_scale(key, extent, split, least, high):
    def one(position, shards_of):
        draws = jax.random.uniform(jax.random.fold_in(jax.random.fold_in(key, 6), position), (shards_of,), jnp.float32, least / len(split), high / len(split))
        return jnp.repeat(jnp.exp(draws), extent[position] // shards_of).reshape((-1,) + (1,) * (len(extent) - position - 1))

    factor_of = one(*split[0])
    for cut in split[1:]:
        factor_of = factor_of * one(*cut)
    return factor_of


def centred(own_key, shape, spread, bound, shards=(), held_as=jnp.bfloat16):
    array = jax.random.normal(own_key, shape, jnp.float32) * spread
    if len(shards) > 0:
        array = block_scale(own_key, shape, shards, -0.22, 0.18) * array
    return jnp.clip(array, min=-bound, max=bound).astype(held_as)


def setup_inputs(seed: int = 0) -> dict:
    splits = jax.random.split(jax.random.key(seed), 5)
    return {
        "inputs": centred(splits[0], (TOKENS, D), 1.0, 6.0, ((0, 32), (1, 16))),
        "w_in": centred(splits[1], (D, FF), D ** -0.5, 0.0546875, ((0, 16), (1, 32))),
        "w_out": centred(splits[2], (FF, D), FF ** -0.5, 0.0390625, ((0, 32), (1, 16))),
        "out_grad": centred(splits[3], (TOKENS, D), 1.0, 6.0, ((0, 32), (1, 16))),
    }


gelu_c = math.sqrt(2.0 / math.pi)

def gelu_parts(pre):
    inner = gelu_c * (pre + 0.044715 * pre * pre * pre)
    tanh_v = jnp.tanh(inner)
    value = 0.5 * pre * (1.0 + tanh_v)
    slope = 0.5 * (1.0 + tanh_v) + 0.5 * pre * (1.0 - tanh_v * tanh_v) * gelu_c * (1.0 + 3.0 * 0.044715 * pre * pre)
    return (value, slope)

def reference(inputs, w_in, w_out, out_grad):
    pre = jnp.dot(inputs, w_in, preferred_element_type=jnp.float32)
    hidden_grad = lax.dot_general(out_grad, w_out, (((1,), (1,)), ((), ())), preferred_element_type=jnp.float32)
    value, slope = gelu_parts(pre)
    hidden = value.astype(jnp.bfloat16)
    pre_grad = (slope * hidden_grad).astype(jnp.bfloat16)
    grad_w_out = lax.dot_general(hidden, out_grad, (((0,), (0,)), ((), ())), preferred_element_type=jnp.float32).astype(jnp.bfloat16)
    grad_w_in = lax.dot_general(inputs, pre_grad, (((0,), (0,)), ((), ())), preferred_element_type=jnp.float32).astype(jnp.bfloat16)
    grad_inputs = lax.dot_general(pre_grad, w_in, (((1,), (1,)), ((), ())), preferred_element_type=jnp.float32).astype(jnp.bfloat16)
    return (grad_inputs, grad_w_in, grad_w_out)
```

```python
import math

import jax
import jax.numpy as jnp
from jax import lax
from jax.experimental import pallas as pl
from jax.experimental.pallas import tpu as pltpu
from jax.sharding import PartitionSpec as P

MESH = pl.DeviceIdType.MESH
BF16, F32 = jnp.bfloat16, jnp.float32
GELU_C = math.sqrt(2.0 / math.pi)

NZ, NYH, NX, NYL = 8, 4, 4, 2
NQ = NX * NYL
TOK = 16
BLK = NYH * TOK
CH = 2 * BLK
NCH = 4
POS = {0: 0, 1: 1, 7: 2, 2: 3, 6: 4, 3: 5, 5: 6, 4: 7}
DIST = {p: d for d, p in POS.items()}
HOPS = [(dx, dy) for dy in range(NYL) for dx in range(NX) if (dx, dy) != (0, 0)]


def activate(pre, hidden_grad):
    inner = GELU_C * (pre + 0.044715 * pre * pre * pre)
    t = jnp.tanh(inner)
    value = 0.5 * pre * (1.0 + t)
    slope = 0.5 * (1.0 + t) + 0.5 * pre * (1.0 - t * t) * GELU_C * (
        1.0 + 3.0 * 0.044715 * pre * pre
    )
    return value.astype(BF16), (slope * hidden_grad).astype(BF16)


def kernel(
    x_hbm, win_hbm, wout_hbm, og_hbm,
    gi_ref, gwin_hbm, gwout_hbm,
    act, win, wout, part, crecv, sendb, own32, rrecv, agall, hid, pg,
    g0, gsend, grecv, ysend, yrecv, gw,
    lsem, ssem, agsem, csem, rsem, zsem, ysem,
):
    row, col = lax.axis_index("row"), lax.axis_index("col")
    core = lax.rem(row, 2)
    x = lax.rem(lax.div(row, 2), NX)
    ylo = lax.div(row, 2 * NX)
    yhi, z = lax.div(col, NZ), lax.rem(col, NZ)
    q = ylo * NX + x
    ncol = win.shape[1]
    half = ncol // NYL

    def at(dx=0, dy=0, dc=0, e=0, d=0):
        r = lax.rem(ylo + dy, NYL) * (2 * NX) + lax.rem(x + dx, NX) * 2 + lax.rem(core + dc, 2)
        c = lax.rem(yhi + e, NYH) * NZ + lax.rem(z + d, NZ)
        return (r, c)

    def chip(dx, dy):
        return lax.rem(ylo + dy, NYL) * NX + lax.rem(x + dx, NX)

    loads = [
        pltpu.make_async_copy(x_hbm, act.at[0, pl.ds(0, TOK)], lsem.at[0]),
        pltpu.make_async_copy(og_hbm, act.at[1, pl.ds(0, TOK)], lsem.at[1]),
        pltpu.make_async_copy(win_hbm, win, lsem.at[2]),
        pltpu.make_async_copy(wout_hbm, wout, lsem.at[3]),
    ]
    for c in loads:
        c.start()
    peers = (
        [at(dc=1)]
        + [at(dx=dx, dy=dy) for dx, dy in HOPS]
        + [at(e=e) for e in range(1, NYH)]
        + [at(d=d) for d in range(1, NZ)]
    )
    barrier = pltpu.get_barrier_semaphore()
    for p in peers:
        pl.semaphore_signal(barrier, inc=1, device_id=p, device_id_type=MESH)
    pl.semaphore_wait(barrier, len(peers))
    loads[0].wait()
    loads[1].wait()

    sent = []

    def send(src, dst, recv_sem, device):
        c = pltpu.make_async_remote_copy(
            src_ref=src, dst_ref=dst, send_sem=ssem.at[len(sent)], recv_sem=recv_sem,
            device_id=device, device_id_type=MESH,
        )
        c.start()
        sent.append(c)

    def arrived(ref, sem):
        pltpu.make_async_copy(ref, ref, sem).wait()

    def piece(d, e):
        return act.at[:, pl.ds(POS[d] * BLK + e * TOK, TOK)]

    def half_piece(a, d, e):
        return act.at[a, pl.ds(POS[d] * BLK + e * TOK, TOK)]

    down, up = at(d=NZ - 1), at(d=1)

    def forward(d, e):
        if d < 3:
            send(piece(d, e), piece(d + 1, e), agsem.at[POS[d + 1], e], down)
        if d == 3:
            send(half_piece(0, 3, e), half_piece(0, 4, e), agsem.at[POS[4], e], down)
        if d == 0 or d > 5:
            to = (d - 1) % NZ
            send(piece(d, e), piece(to, e), agsem.at[POS[to], e], up)
        if d == 5:
            send(half_piece(1, 5, e), half_piece(1, 4, e), agsem.at[NZ, e], up)

    def take(d, e):
        if d == 4:
            arrived(half_piece(0, 4, e), agsem.at[POS[4], e])
            arrived(half_piece(1, 4, e), agsem.at[NZ, e])
        else:
            arrived(piece(d, e), agsem.at[POS[d], e])
            forward(d, e)

    def take_ring(i, e):
        take(i, e)
        take(NZ - i, e)

    def multiply(ci):
        rows = pl.ds(ci * CH, CH)
        pre = jnp.dot(act[0, rows], win[...], preferred_element_type=F32)
        part[ci, 0, 0] = pre[:BLK]
        part[ci, 1, 0] = pre[BLK:]
        hg = lax.dot_general(
            act[1, rows], wout[...], (((1,), (1,)), ((), ())), preferred_element_type=F32
        )
        part[ci, 0, 1] = hg[:BLK]
        part[ci, 1, 1] = hg[BLK:]
        send(part.at[ci, 1 - core], crecv.at[ci], csem.at[0, ci], at(dc=1))

    def scatter(ci):
        arrived(crecv.at[ci], csem.at[0, ci])
        for k in range(NQ):
            r, c = pl.ds((k % NX) * TOK, TOK), pl.ds((k // NX) * half, half)
            total = part[ci, core, :, r, c] + crecv[ci, :, r, c]
            own32[ci, k] = total
            sendb[ci, k] = total.astype(BF16)
        for k, (dx, dy) in enumerate(HOPS):
            send(sendb.at[ci, chip(dx, dy)], rrecv.at[ci, k], rsem.at[0, ci], at(dx=dx, dy=dy))

    def activation(ci):
        arrived(rrecv.at[ci], rsem.at[0, ci])
        total = own32[ci, q]
        for k in range(NQ - 1):
            total = total + rrecv[ci, k].astype(F32)
        value, slope = activate(total[0], total[1])
        agall[ci, core, q, 0] = value
        agall[ci, core, q, 1] = slope
        for dx, dy in HOPS:
            send(agall.at[ci, core, q], agall.at[ci, core, q], rsem.at[1, ci], at(dx=dx, dy=dy))

    def share(ci):
        arrived(rrecv.at[ci], rsem.at[1, ci])
        send(agall.at[ci, core], agall.at[ci, core], csem.at[1, ci], at(dc=1))

    def back(ci):
        arrived(agall.at[ci, 0], csem.at[1, ci])
        for h in range(2):
            for k in range(NQ):
                r = pl.ds(ci * CH + h * BLK + (k % NX) * TOK, TOK)
                c = pl.ds((k // NX) * half, half)
                hid[r, c] = agall[ci, h, k, 0]
                pg[r, c] = agall[ci, h, k, 1]
        g = lax.dot_general(
            pg[pl.ds(ci * CH, CH)], win[...], (((1,), (1,)), ((), ())), preferred_element_type=F32
        )
        for h in range(2):
            d = DIST[2 * ci + h]
            block = g[h * BLK:(h + 1) * BLK]
            if d == 0:
                g0[...] = block
            else:
                gsend[d] = block.astype(BF16)
                send(gsend.at[d], grecv.at[d], zsem.at[d], at(d=d))

    def weight_grads():
        out = []
        for a, (lhs, rhs, dst) in enumerate(
            ((hid, act.at[1], gwout_hbm), (act.at[0], pg, gwin_hbm))
        ):
            step = 256
            for i in range(lhs.shape[1] // step):
                r = pl.ds(i * step, step)
                gw[a, r] = lax.dot_general(
                    lhs[:, r], rhs[...], (((0,), (0,)), ((), ())), preferred_element_type=F32
                ).astype(BF16)
                c = pltpu.make_async_copy(gw.at[a, r], dst.at[r], lsem.at[4 + a * 3 + i])
                c.start()
                out.append(c)
        return out

    forward(0, 0)
    for e in (1, 3, 2):
        send(piece(0, 0), piece(0, e), agsem.at[0, e], at(e=NYH - e))
    for e in (1, 3):
        take(0, e)
    take_ring(1, 0)
    take(0, 2)
    for e in (1, 3):
        take_ring(1, e)
    take_ring(2, 0)
    take_ring(1, 2)
    loads[2].wait()
    loads[3].wait()
    multiply(0)
    for e in (1, 3):
        take_ring(2, e)
    scatter(0)
    take_ring(3, 0)
    take_ring(2, 2)
    multiply(1)
    for e in (1, 3):
        take_ring(3, e)
    scatter(1)
    take_ring(3, 2)
    multiply(2)
    activation(0)
    scatter(2)
    for e in (0, 1, 3, 2):
        take(4, e)
    multiply(3)
    activation(1)
    scatter(3)
    share(0)
    activation(2)
    back(0)
    share(1)
    activation(3)
    back(1)
    share(2)
    back(2)
    share(3)
    back(3)
    stores = weight_grads()
    total = g0[...]
    for d in range(1, NZ):
        arrived(grecv.at[d], zsem.at[d])
        total = total + grecv[d].astype(F32)
    for e in range(NYH):
        ysend[e] = total[e * TOK:(e + 1) * TOK]
    for e in range(1, NYH):
        send(ysend.at[e], yrecv.at[e], ysem.at[e], at(e=e))
    total = ysend[0]
    for e in range(1, NYH):
        arrived(yrecv.at[e], ysem.at[e])
        total = total + yrecv[e]
    gi_ref[...] = total.astype(BF16)
    for c in sent:
        c.wait_send()
    for c in stores:
        c.wait()


N_SENDS = 32 + 3 + 2 * NCH + 2 * 7 * NCH + (NZ - 1) + (NYH - 1)


def local(inputs, w_in, w_out, out_grad):
    feat, ff = w_in.shape
    half = ff // NYL
    tokens = TOK * NYH * NZ
    any_spec = pl.BlockSpec(memory_space=pl.ANY)
    vmem = pltpu.VMEM
    return pl.pallas_call(
        kernel,
        out_shape=(
            jax.ShapeDtypeStruct(inputs.shape, BF16),
            jax.ShapeDtypeStruct(w_in.shape, BF16),
            jax.ShapeDtypeStruct(w_out.shape, BF16),
        ),
        in_specs=[any_spec] * 4,
        out_specs=(pl.BlockSpec(memory_space=pltpu.VMEM), any_spec, any_spec),
        scratch_shapes=[
            vmem((2, tokens, feat), BF16),
            vmem((feat, ff), BF16),
            vmem((ff, feat), BF16),
            vmem((NCH, 2, 2, BLK, ff), F32),
            vmem((NCH, 2, BLK, ff), F32),
            vmem((NCH, NQ, 2, TOK, half), BF16),
            vmem((NCH, NQ, 2, TOK, half), F32),
            vmem((NCH, NQ - 1, 2, TOK, half), BF16),
            vmem((NCH, 2, NQ, 2, TOK, half), BF16),
            vmem((tokens, ff), BF16),
            vmem((tokens, ff), BF16),
            vmem((BLK, feat), F32),
            vmem((NZ, BLK, feat), BF16),
            vmem((NZ, BLK, feat), BF16),
            vmem((NYH, TOK, feat), F32),
            vmem((NYH, TOK, feat), F32),
            vmem((2, feat, ff), BF16),
            pltpu.SemaphoreType.DMA((10,)),
            pltpu.SemaphoreType.DMA((N_SENDS,)),
            pltpu.SemaphoreType.DMA((NZ + 1, NYH)),
            pltpu.SemaphoreType.DMA((2, NCH)),
            pltpu.SemaphoreType.DMA((2, NCH)),
            pltpu.SemaphoreType.DMA((NZ,)),
            pltpu.SemaphoreType.DMA((NYH,)),
        ],
        compiler_params=pltpu.CompilerParams(
            collective_id=0, has_side_effects=True, vmem_limit_bytes=48 * 2**20
        ),
        cost_estimate=pl.CostEstimate(
            flops=10 * tokens * feat * ff, bytes_accessed=8 * feat * ff, transcendentals=0
        ),
    )(inputs, w_in, w_out, out_grad)


def solution(mesh):
    return jax.shard_map(
        local,
        mesh=mesh,
        in_specs=(P("col", "row"), P("row", "col"), P("col", "row"), P("col", "row")),
        out_specs=(P("col", "row"), P("row", "col"), P("col", "row")),
        check_vma=False,
    )
```

```python
import math

import jax
import jax.numpy as jnp
from jax import lax
from jax.experimental import pallas as pl
from jax.experimental.pallas import tpu as pltpu
from jax.sharding import PartitionSpec as P

MESH = pl.DeviceIdType.MESH
BF16, F32 = jnp.bfloat16, jnp.float32
GELU_C = math.sqrt(2.0 / math.pi)

NZ, NYH, NX, NYL = 8, 4, 4, 2
NQ = NX * NYL
TOK = 16
BLK = NYH * TOK
CH = 2 * BLK
NCH = 4
TILE = 256
POS = {0: 0, 1: 1, 7: 2, 2: 3, 6: 4, 3: 5, 5: 6, 4: 7}
DIST = {p: d for d, p in POS.items()}
NEAR, FAR = (1, 7, 2, 6), (3, 5, 4)
HOPS = [(dx, dy) for dy in range(NYL) for dx in range(NX) if (dx, dy) != (0, 0)]

ORDER = [
    ("start",), ("ring", 1, 0), ("take", 0, 1), ("take", 0, 3), ("ring", 2, 0), ("take", 0, 2),
    ("ring", 1, 1), ("ring", 1, 3), ("ring", 3, 0), ("ring", 1, 2),
    ("weights",), ("mul", 0), ("ring", 2, 1), ("ring", 2, 3), ("scatter", 0),
    ("ring", 2, 2), ("mul", 1), ("ring", 3, 1), ("ring", 3, 3), ("scatter", 1),
    ("take", 4, 0), ("ring", 3, 2), ("mul", 2), ("act", 0), ("scatter", 2),
    ("take", 4, 1), ("take", 4, 3), ("take", 4, 2), ("mul", 3), ("act", 1), ("scatter", 3),
    ("share", 0), ("act", 2), ("back", 0), ("share", 1), ("act", 3), ("back", 1),
    ("share", 2), ("back", 2), ("share", 3), ("back", 3), ("far", 3), ("grads", 0), ("near",),
    ("far", 5), ("far", 4), ("grads", 1), ("end",),
]


def activate(pre, hidden_grad):
    inner = GELU_C * (pre + 0.044715 * pre * pre * pre)
    t = jnp.tanh(inner)
    value = 0.5 * pre * (1.0 + t)
    slope = 0.5 * (1.0 + t) + 0.5 * pre * (1.0 - t * t) * GELU_C * (
        1.0 + 3.0 * 0.044715 * pre * pre
    )
    return value.astype(BF16), (slope * hidden_grad).astype(BF16)


def kernel(
    x_hbm, win_hbm, wout_hbm, og_hbm,
    gi_ref, gwin_hbm, gwout_hbm,
    act, win, wout, part, crecv, sendb, own32, rrecv, agall, hid, pg,
    g0, gsend, grecv, f0, fsend, frecv, tsend, trecv, y0, ysend, yrecv, gw,
    lsem, ssem, agsem, csem, rsem, zsem, fsem, tsem, ysem,
):
    row, col = lax.axis_index("row"), lax.axis_index("col")
    core = lax.rem(row, 2)
    x = lax.rem(lax.div(row, 2), NX)
    ylo = lax.div(row, 2 * NX)
    yhi, z = lax.div(col, NZ), lax.rem(col, NZ)
    q = ylo * NX + x
    ncol = win.shape[1]
    half = ncol // NYL

    def at(dx=0, dy=0, dc=0, e=0, d=0):
        r = lax.rem(ylo + dy, NYL) * (2 * NX) + lax.rem(x + dx, NX) * 2 + lax.rem(core + dc, 2)
        c = lax.rem(yhi + e, NYH) * NZ + lax.rem(z + d, NZ)
        return (r, c)

    def chip(dx, dy):
        return lax.rem(ylo + dy, NYL) * NX + lax.rem(x + dx, NX)

    loads = [
        pltpu.make_async_copy(x_hbm, act.at[0, pl.ds(0, TOK)], lsem.at[0]),
        pltpu.make_async_copy(og_hbm, act.at[1, pl.ds(0, TOK)], lsem.at[1]),
        pltpu.make_async_copy(win_hbm, win, lsem.at[2]),
        pltpu.make_async_copy(wout_hbm, wout, lsem.at[3]),
    ]
    for c in loads:
        c.start()
    peers = (
        [at(dc=1)]
        + [at(dx=dx, dy=dy) for dx, dy in HOPS]
        + [at(e=e) for e in range(1, NYH)]
        + [at(d=d) for d in range(1, NZ)]
    )
    barrier = pltpu.get_barrier_semaphore()
    for p in peers:
        pl.semaphore_signal(barrier, inc=1, device_id=p, device_id_type=MESH)
    pl.semaphore_wait(barrier, len(peers))
    loads[0].wait()
    loads[1].wait()

    sent = []

    def send(src, dst, recv_sem, device):
        c = pltpu.make_async_remote_copy(
            src_ref=src, dst_ref=dst, send_sem=ssem.at[len(sent)], recv_sem=recv_sem,
            device_id=device, device_id_type=MESH,
        )
        c.start()
        sent.append(c)

    def arrived(ref, sem):
        pltpu.make_async_copy(ref, ref, sem).wait()

    def piece(d, e):
        return act.at[:, pl.ds(POS[d] * BLK + e * TOK, TOK)]

    def half_piece(a, d, e):
        return act.at[a, pl.ds(POS[d] * BLK + e * TOK, TOK)]

    down, up = at(d=NZ - 1), at(d=1)

    def forward(d, e):
        if d < 3:
            send(piece(d, e), piece(d + 1, e), agsem.at[POS[d + 1], e], down)
        if d == 3:
            send(half_piece(0, 3, e), half_piece(0, 4, e), agsem.at[POS[4], e], down)
        if d == 0 or d > 5:
            to = (d - 1) % NZ
            send(piece(d, e), piece(to, e), agsem.at[POS[to], e], up)
        if d == 5:
            send(half_piece(1, 5, e), half_piece(1, 4, e), agsem.at[NZ, e], up)

    def take(d, e):
        if d == 4:
            arrived(half_piece(0, 4, e), agsem.at[POS[4], e])
            arrived(half_piece(1, 4, e), agsem.at[NZ, e])
        else:
            arrived(piece(d, e), agsem.at[POS[d], e])
            forward(d, e)

    def take_ring(i, e):
        take(i, e)
        take(NZ - i, e)

    def multiply(ci):
        rows = pl.ds(ci * CH, CH)
        pre = jnp.dot(act[0, rows], win[...], preferred_element_type=F32)
        part[ci, 0, 0] = pre[:BLK]
        part[ci, 1, 0] = pre[BLK:]
        hg = lax.dot_general(
            act[1, rows], wout[...], (((1,), (1,)), ((), ())), preferred_element_type=F32
        )
        part[ci, 0, 1] = hg[:BLK]
        part[ci, 1, 1] = hg[BLK:]
        send(part.at[ci, 1 - core], crecv.at[ci], csem.at[0, ci], at(dc=1))

    def scatter(ci):
        arrived(crecv.at[ci], csem.at[0, ci])
        for k in range(NQ):
            r, c = pl.ds((k % NX) * TOK, TOK), pl.ds((k // NX) * half, half)
            total = part[ci, core, :, r, c] + crecv[ci, :, r, c]
            own32[ci, k] = total
            sendb[ci, k] = total.astype(BF16)
        for k, (dx, dy) in enumerate(HOPS):
            send(sendb.at[ci, chip(dx, dy)], rrecv.at[ci, k], rsem.at[0, ci], at(dx=dx, dy=dy))

    def activation(ci):
        arrived(rrecv.at[ci], rsem.at[0, ci])
        total = own32[ci, q]
        for k in range(NQ - 1):
            total = total + rrecv[ci, k].astype(F32)
        value, slope = activate(total[0], total[1])
        agall[ci, core, q, 0] = value
        agall[ci, core, q, 1] = slope
        for dx, dy in HOPS:
            send(agall.at[ci, core, q], agall.at[ci, core, q], rsem.at[1, ci], at(dx=dx, dy=dy))

    def share(ci):
        arrived(rrecv.at[ci], rsem.at[1, ci])
        send(agall.at[ci, core], agall.at[ci, core], csem.at[1, ci], at(dc=1))

    def back(ci):
        arrived(agall.at[ci, 0], csem.at[1, ci])
        for h in range(2):
            for k in range(NQ):
                r = pl.ds(ci * CH + h * BLK + (k % NX) * TOK, TOK)
                c = pl.ds((k // NX) * half, half)
                hid[r, c] = agall[ci, h, k, 0]
                pg[r, c] = agall[ci, h, k, 1]
        g = lax.dot_general(
            pg[pl.ds(ci * CH, CH)], win[...], (((1,), (1,)), ((), ())), preferred_element_type=F32
        )
        for h in range(2):
            d = DIST[2 * ci + h]
            block = g[h * BLK:(h + 1) * BLK]
            if d == 0:
                g0[...] = block
            elif d in NEAR:
                i = NEAR.index(d)
                gsend[i] = block.astype(BF16)
                send(gsend.at[i], grecv.at[i], zsem.at[i], at(d=d))
            else:
                i = FAR.index(d)
                f0[i] = block[:TOK]
                fsend[i] = block[TOK:].astype(BF16).reshape(fsend.shape[1:])
                for e in range(1, NYH):
                    send(fsend.at[i, e - 1], frecv.at[i, e - 1], fsem.at[i], at(e=e))

    def far(d):
        i = FAR.index(d)
        arrived(frecv.at[i], fsem.at[i])
        total = f0[i]
        for e in range(NYH - 1):
            total = total + frecv[i, e].astype(F32)
        tsend[i] = total.astype(BF16)
        send(tsend.at[i], trecv.at[i], tsem.at[i], at(d=d))

    def weight_grads(a):
        lhs, rhs, dst = ((hid, act.at[1], gwout_hbm), (act.at[0], pg, gwin_hbm))[a]
        for i in range(lhs.shape[1] // TILE):
            r = pl.ds(i * TILE, TILE)
            gw[a, r] = lax.dot_general(
                lhs[:, r], rhs[...], (((0,), (0,)), ((), ())), preferred_element_type=F32
            ).astype(BF16)
            c = pltpu.make_async_copy(gw.at[a, r], dst.at[r], lsem.at[4 + a * 3 + i])
            c.start()
            stores.append(c)

    def gather_start():
        forward(0, 0)
        for e in (1, 3, 2):
            send(piece(0, 0), piece(0, e), agsem.at[0, e], at(e=NYH - e))

    def weights_ready():
        loads[2].wait()
        loads[3].wait()

    stores = []

    def near():
        total = g0[...]
        for i in range(len(NEAR)):
            arrived(grecv.at[i], zsem.at[i])
            total = total + grecv[i].astype(F32)
        y0[...] = total[:TOK]
        ysend[...] = total[TOK:].astype(BF16).reshape(ysend.shape)
        for e in range(1, NYH):
            send(ysend.at[e - 1], yrecv.at[e - 1], ysem.at[0], at(e=e))

    def finish():
        total = y0[...]
        arrived(yrecv, ysem.at[0])
        for e in range(NYH - 1):
            total = total + yrecv[e].astype(F32)
        for i in range(len(FAR)):
            arrived(trecv.at[i], tsem.at[i])
            total = total + trecv[i].astype(F32)
        gi_ref[...] = total.astype(BF16)

    steps = {
        "start": gather_start, "take": take, "ring": take_ring, "weights": weights_ready,
        "mul": multiply, "scatter": scatter, "act": activation, "share": share, "back": back,
        "far": far, "grads": weight_grads, "near": near, "end": finish,
    }
    for name, *args in ORDER:
        steps[name](*args)
    for c in sent:
        c.wait_send()
    for c in stores:
        c.wait()


N_SENDS = 32 + 3 + 2 * NCH + 2 * 7 * NCH + len(NEAR) + 4 * len(FAR) + (NYH - 1)


def local(inputs, w_in, w_out, out_grad):
    feat, ff = w_in.shape
    half = ff // NYL
    tokens = TOK * NYH * NZ
    any_spec = pl.BlockSpec(memory_space=pl.ANY)
    vmem = pltpu.VMEM
    return pl.pallas_call(
        kernel,
        out_shape=(
            jax.ShapeDtypeStruct(inputs.shape, BF16),
            jax.ShapeDtypeStruct(w_in.shape, BF16),
            jax.ShapeDtypeStruct(w_out.shape, BF16),
        ),
        in_specs=[any_spec] * 4,
        out_specs=(pl.BlockSpec(memory_space=pltpu.VMEM), any_spec, any_spec),
        scratch_shapes=[
            vmem((2, tokens, feat), BF16),
            vmem((feat, ff), BF16),
            vmem((ff, feat), BF16),
            vmem((NCH, 2, 2, BLK, ff), F32),
            vmem((NCH, 2, BLK, ff), F32),
            vmem((NCH, NQ, 2, TOK, half), BF16),
            vmem((NCH, NQ, 2, TOK, half), F32),
            vmem((NCH, NQ - 1, 2, TOK, half), BF16),
            vmem((NCH, 2, NQ, 2, TOK, half), BF16),
            vmem((tokens, ff), BF16),
            vmem((tokens, ff), BF16),
            vmem((BLK, feat), F32),
            vmem((len(NEAR), BLK, feat), BF16),
            vmem((len(NEAR), BLK, feat), BF16),
            vmem((len(FAR), TOK, feat), F32),
            vmem((len(FAR), NYH - 1, TOK, feat), BF16),
            vmem((len(FAR), NYH - 1, TOK, feat), BF16),
            vmem((len(FAR), TOK, feat), BF16),
            vmem((len(FAR), TOK, feat), BF16),
            vmem((TOK, feat), F32),
            vmem((NYH - 1, TOK, feat), BF16),
            vmem((NYH - 1, TOK, feat), BF16),
            vmem((2, feat, ff), BF16),
            pltpu.SemaphoreType.DMA((10,)),
            pltpu.SemaphoreType.DMA((N_SENDS,)),
            pltpu.SemaphoreType.DMA((NZ + 1, NYH)),
            pltpu.SemaphoreType.DMA((2, NCH)),
            pltpu.SemaphoreType.DMA((2, NCH)),
            pltpu.SemaphoreType.DMA((len(NEAR),)),
            pltpu.SemaphoreType.DMA((len(FAR),)),
            pltpu.SemaphoreType.DMA((len(FAR),)),
            pltpu.SemaphoreType.DMA((1,)),
        ],
        compiler_params=pltpu.CompilerParams(
            collective_id=0, has_side_effects=True, vmem_limit_bytes=56 * 2**20
        ),
        cost_estimate=pl.CostEstimate(
            flops=10 * tokens * feat * ff, bytes_accessed=8 * feat * ff, transcendentals=0
        ),
    )(inputs, w_in, w_out, out_grad)


def solution(mesh):
    return jax.shard_map(
        local,
        mesh=mesh,
        in_specs=(P("col", "row"), P("row", "col"), P("col", "row"), P("col", "row")),
        out_specs=(P("col", "row"), P("row", "col"), P("col", "row")),
        check_vma=False,
    )
```

```python
import math

import jax
import jax.numpy as jnp
from jax import lax
from jax.experimental import pallas as pl
from jax.experimental.pallas import tpu as pltpu
from jax.sharding import PartitionSpec as P

MESH = pl.DeviceIdType.MESH
BF16, F32 = jnp.bfloat16, jnp.float32
GELU_C = math.sqrt(2.0 / math.pi)

NZ, NYH, NX, NYL = 8, 4, 4, 2
NQ = NX * NYL
TOK = 16
BLK = NYH * TOK
CH = 2 * BLK
NCH = 4
TILE = 256
POS = {1: 0, 7: 1, 2: 2, 6: 3, 3: 4, 5: 5, 0: 6, 4: 7}
DIST = {p: d for d, p in POS.items()}
NEAR, FAR = (1, 7, 2, 6), (3, 5, 4)
YHOPS = [2, 1, 3]
HOPS = [(2, 1), (2, 0), (1, 1), (3, 1), (1, 0), (3, 0), (0, 1)]

ORDER = [
    ("start",), ("ring", 1, 0), ("take", 0, 3), ("take", 0, 1), ("take", 0, 2), ("ring", 1, 3),
    ("ring", 1, 1), ("ring", 1, 2), ("ring", 2, 0), ("weights",), ("mul", 0), ("ring", 2, 3),
    ("ring", 2, 1), ("scatter", 0), ("ring", 2, 2), ("mul", 1), ("ring", 3, 3), ("ring", 3, 0),
    ("scatter", 1), ("ring", 3, 1), ("ring", 3, 2), ("mul", 2), ("act", 0), ("take", 4, 0),
    ("scatter", 2), ("take", 4, 1), ("take", 4, 2), ("take", 4, 3), ("mul", 3), ("scatter", 3),
    ("act", 2), ("act", 1), ("share", 0), ("act", 3), ("back", 0), ("share", 2), ("back", 2),
    ("share", 1), ("share", 3), ("back", 1), ("back", 3), ("far", 3), ("far", 5), ("far", 4),
    ("near",), ("grads", 1), ("grads", 0), ("end",),
]


def activate(pre, hidden_grad):
    inner = GELU_C * (pre + 0.044715 * pre * pre * pre)
    t = jnp.tanh(inner)
    value = 0.5 * pre * (1.0 + t)
    slope = 0.5 * (1.0 + t) + 0.5 * pre * (1.0 - t * t) * GELU_C * (
        1.0 + 3.0 * 0.044715 * pre * pre
    )
    return value.astype(BF16), (slope * hidden_grad).astype(BF16)


def kernel(
    x_hbm, win_hbm, wout_hbm, og_hbm,
    gi_ref, gwin_hbm, gwout_hbm,
    act, win, wout, part, crecv, sendb, own32, rrecv, agall, hid, pg,
    g0, gsend, grecv, f0, fsend, frecv, tsend, trecv, y0, ysend, yrecv, gw,
    lsem, ssem, agsem, csem, rsem, zsem, fsem, tsem, ysem,
):
    row, col = lax.axis_index("row"), lax.axis_index("col")
    core = lax.rem(row, 2)
    x = lax.rem(lax.div(row, 2), NX)
    ylo = lax.div(row, 2 * NX)
    yhi, z = lax.div(col, NZ), lax.rem(col, NZ)
    q = ylo * NX + x
    ncol = win.shape[1]
    half = ncol // NYL

    def at(dx=0, dy=0, dc=0, e=0, d=0):
        r = lax.rem(ylo + dy, NYL) * (2 * NX) + lax.rem(x + dx, NX) * 2 + lax.rem(core + dc, 2)
        c = lax.rem(yhi + e, NYH) * NZ + lax.rem(z + d, NZ)
        return (r, c)

    def chip(dx, dy):
        return lax.rem(ylo + dy, NYL) * NX + lax.rem(x + dx, NX)

    own = pl.ds(POS[0] * BLK, TOK)
    loads = [
        pltpu.make_async_copy(x_hbm, act.at[0, own], lsem.at[0]),
        pltpu.make_async_copy(og_hbm, act.at[1, own], lsem.at[1]),
        pltpu.make_async_copy(win_hbm, win, lsem.at[2]),
        pltpu.make_async_copy(wout_hbm, wout, lsem.at[3]),
    ]
    for c in loads:
        c.start()
    peers = (
        [at(dc=1)]
        + [at(dx=dx, dy=dy) for dx, dy in HOPS]
        + [at(e=e) for e in range(1, NYH)]
        + [at(d=d) for d in range(1, NZ)]
    )
    barrier = pltpu.get_barrier_semaphore()
    for p in peers:
        pl.semaphore_signal(barrier, inc=1, device_id=p, device_id_type=MESH)
    pl.semaphore_wait(barrier, len(peers))
    loads[0].wait()
    loads[1].wait()

    sent = []

    def send(src, dst, recv_sem, device):
        c = pltpu.make_async_remote_copy(
            src_ref=src, dst_ref=dst, send_sem=ssem.at[len(sent)], recv_sem=recv_sem,
            device_id=device, device_id_type=MESH,
        )
        c.start()
        sent.append(c)

    def arrived(ref, sem):
        pltpu.make_async_copy(ref, ref, sem).wait()

    def piece(d, e):
        return act.at[:, pl.ds(POS[d] * BLK + e * TOK, TOK)]

    def half_piece(a, d, e):
        return act.at[a, pl.ds(POS[d] * BLK + e * TOK, TOK)]

    down, up = at(d=NZ - 1), at(d=1)

    def forward(d, e):
        if d < 3:
            send(piece(d, e), piece(d + 1, e), agsem.at[POS[d + 1], e], down)
        if d == 3:
            send(half_piece(0, 3, e), half_piece(0, 4, e), agsem.at[POS[4], e], down)
        if d == 0 or d > 5:
            to = (d - 1) % NZ
            send(piece(d, e), piece(to, e), agsem.at[POS[to], e], up)
        if d == 5:
            send(half_piece(1, 5, e), half_piece(1, 4, e), agsem.at[NZ, e], up)

    def take(d, e):
        if d == 4:
            arrived(half_piece(0, 4, e), agsem.at[POS[4], e])
            arrived(half_piece(1, 4, e), agsem.at[NZ, e])
        else:
            arrived(piece(d, e), agsem.at[POS[d], e])
            forward(d, e)

    def take_ring(i, e):
        take(i, e)
        take(NZ - i, e)

    def multiply(ci):
        rows = pl.ds(ci * CH, CH)
        pre = jnp.dot(act[0, rows], win[...], preferred_element_type=F32)
        part[ci, 0, 0] = pre[:BLK]
        part[ci, 1, 0] = pre[BLK:]
        hg = lax.dot_general(
            act[1, rows], wout[...], (((1,), (1,)), ((), ())), preferred_element_type=F32
        )
        part[ci, 0, 1] = hg[:BLK]
        part[ci, 1, 1] = hg[BLK:]
        send(part.at[ci, 1 - core], crecv.at[ci], csem.at[0, ci], at(dc=1))

    def scatter(ci):
        arrived(crecv.at[ci], csem.at[0, ci])
        for k in range(NQ):
            r, c = pl.ds((k % NX) * TOK, TOK), pl.ds((k // NX) * half, half)
            total = part[ci, core, :, r, c] + crecv[ci, :, r, c]
            own32[ci, k] = total
            sendb[ci, k] = total.astype(BF16)
        for k, (dx, dy) in enumerate(HOPS):
            send(sendb.at[ci, chip(dx, dy)], rrecv.at[ci, k], rsem.at[0, ci], at(dx=dx, dy=dy))

    def activation(ci):
        arrived(rrecv.at[ci], rsem.at[0, ci])
        total = own32[ci, q]
        for k in range(NQ - 1):
            total = total + rrecv[ci, k].astype(F32)
        value, slope = activate(total[0], total[1])
        agall[ci, core, q, 0] = value
        agall[ci, core, q, 1] = slope
        for dx, dy in HOPS:
            send(agall.at[ci, core, q], agall.at[ci, core, q], rsem.at[1, ci], at(dx=dx, dy=dy))

    def share(ci):
        arrived(rrecv.at[ci], rsem.at[1, ci])
        send(agall.at[ci, core], agall.at[ci, core], csem.at[1, ci], at(dc=1))

    def back(ci):
        arrived(agall.at[ci, 0], csem.at[1, ci])
        for h in range(2):
            for k in range(NQ):
                r = pl.ds(ci * CH + h * BLK + (k % NX) * TOK, TOK)
                c = pl.ds((k // NX) * half, half)
                hid[r, c] = agall[ci, h, k, 0]
                pg[r, c] = agall[ci, h, k, 1]
        g = lax.dot_general(
            pg[pl.ds(ci * CH, CH)], win[...], (((1,), (1,)), ((), ())), preferred_element_type=F32
        )
        for h in range(2):
            d = DIST[2 * ci + h]
            block = g[h * BLK:(h + 1) * BLK]
            if d == 0:
                g0[...] = block
            elif d in NEAR:
                i = NEAR.index(d)
                gsend[i] = block.astype(BF16)
                send(gsend.at[i], grecv.at[i], zsem.at[i], at(d=d))
            else:
                i = FAR.index(d)
                f0[i] = block[:TOK]
                fsend[i] = block[TOK:].astype(BF16).reshape(fsend.shape[1:])
                for e in YHOPS:
                    send(fsend.at[i, e - 1], frecv.at[i, e - 1], fsem.at[i], at(e=e))

    def far(d):
        i = FAR.index(d)
        arrived(frecv.at[i], fsem.at[i])
        total = f0[i]
        for e in range(NYH - 1):
            total = total + frecv[i, e].astype(F32)
        tsend[i] = total.astype(BF16)
        send(tsend.at[i], trecv.at[i], tsem.at[i], at(d=d))

    def weight_grads(a):
        lhs, rhs, dst = ((hid, act.at[1], gwout_hbm), (act.at[0], pg, gwin_hbm))[a]
        for i in range(lhs.shape[1] // TILE):
            r = pl.ds(i * TILE, TILE)
            gw[a, r] = lax.dot_general(
                lhs[:, r], rhs[...], (((0,), (0,)), ((), ())), preferred_element_type=F32
            ).astype(BF16)
            c = pltpu.make_async_copy(gw.at[a, r], dst.at[r], lsem.at[4 + a * 3 + i])
            c.start()
            stores.append(c)

    def gather_start():
        forward(0, 0)
        for e in YHOPS:
            send(piece(0, 0), piece(0, e), agsem.at[POS[0], e], at(e=NYH - e))

    def weights_ready():
        loads[2].wait()
        loads[3].wait()

    stores = []

    def near():
        total = g0[...]
        for i in range(len(NEAR)):
            arrived(grecv.at[i], zsem.at[i])
            total = total + grecv[i].astype(F32)
        y0[...] = total[:TOK]
        ysend[...] = total[TOK:].astype(BF16).reshape(ysend.shape)
        for e in YHOPS:
            send(ysend.at[e - 1], yrecv.at[e - 1], ysem.at[0], at(e=e))

    def finish():
        total = y0[...]
        arrived(yrecv, ysem.at[0])
        for e in range(NYH - 1):
            total = total + yrecv[e].astype(F32)
        for i in range(len(FAR)):
            arrived(trecv.at[i], tsem.at[i])
            total = total + trecv[i].astype(F32)
        gi_ref[...] = total.astype(BF16)

    steps = {
        "start": gather_start, "take": take, "ring": take_ring, "weights": weights_ready,
        "mul": multiply, "scatter": scatter, "act": activation, "share": share, "back": back,
        "far": far, "grads": weight_grads, "near": near, "end": finish,
    }
    for name, *args in ORDER:
        steps[name](*args)
    for c in sent:
        c.wait_send()
    for c in stores:
        c.wait()


N_SENDS = 32 + 3 + 2 * NCH + 2 * 7 * NCH + len(NEAR) + 4 * len(FAR) + (NYH - 1)


def local(inputs, w_in, w_out, out_grad):
    feat, ff = w_in.shape
    half = ff // NYL
    tokens = TOK * NYH * NZ
    any_spec = pl.BlockSpec(memory_space=pl.ANY)
    vmem = pltpu.VMEM
    return pl.pallas_call(
        kernel,
        out_shape=(
            jax.ShapeDtypeStruct(inputs.shape, BF16),
            jax.ShapeDtypeStruct(w_in.shape, BF16),
            jax.ShapeDtypeStruct(w_out.shape, BF16),
        ),
        in_specs=[any_spec] * 4,
        out_specs=(pl.BlockSpec(memory_space=pltpu.VMEM), any_spec, any_spec),
        scratch_shapes=[
            vmem((2, tokens, feat), BF16),
            vmem((feat, ff), BF16),
            vmem((ff, feat), BF16),
            vmem((NCH, 2, 2, BLK, ff), F32),
            vmem((NCH, 2, BLK, ff), F32),
            vmem((NCH, NQ, 2, TOK, half), BF16),
            vmem((NCH, NQ, 2, TOK, half), F32),
            vmem((NCH, NQ - 1, 2, TOK, half), BF16),
            vmem((NCH, 2, NQ, 2, TOK, half), BF16),
            vmem((tokens, ff), BF16),
            vmem((tokens, ff), BF16),
            vmem((BLK, feat), F32),
            vmem((len(NEAR), BLK, feat), BF16),
            vmem((len(NEAR), BLK, feat), BF16),
            vmem((len(FAR), TOK, feat), F32),
            vmem((len(FAR), NYH - 1, TOK, feat), BF16),
            vmem((len(FAR), NYH - 1, TOK, feat), BF16),
            vmem((len(FAR), TOK, feat), BF16),
            vmem((len(FAR), TOK, feat), BF16),
            vmem((TOK, feat), F32),
            vmem((NYH - 1, TOK, feat), BF16),
            vmem((NYH - 1, TOK, feat), BF16),
            vmem((2, feat, ff), BF16),
            pltpu.SemaphoreType.DMA((10,)),
            pltpu.SemaphoreType.DMA((N_SENDS,)),
            pltpu.SemaphoreType.DMA((NZ + 1, NYH)),
            pltpu.SemaphoreType.DMA((2, NCH)),
            pltpu.SemaphoreType.DMA((2, NCH)),
            pltpu.SemaphoreType.DMA((len(NEAR),)),
            pltpu.SemaphoreType.DMA((len(FAR),)),
            pltpu.SemaphoreType.DMA((len(FAR),)),
            pltpu.SemaphoreType.DMA((1,)),
        ],
        compiler_params=pltpu.CompilerParams(
            collective_id=0, has_side_effects=True, vmem_limit_bytes=48 * 2**20
        ),
        cost_estimate=pl.CostEstimate(
            flops=10 * tokens * feat * ff, bytes_accessed=8 * feat * ff, transcendentals=0
        ),
    )(*(pltpu.with_memory_space_constraint(a, pltpu.HBM) for a in (inputs, w_in, w_out, out_grad)))


def solution(mesh):
    return jax.shard_map(
        local,
        mesh=mesh,
        in_specs=(P("col", "row"), P("row", "col"), P("col", "row"), P("col", "row")),
        out_specs=(P("col", "row"), P("row", "col"), P("col", "row")),
        check_vma=False,
    )
```

```python
import math

import jax
import jax.numpy as jnp
from jax import lax
from jax.experimental import pallas as pl
from jax.experimental.pallas import tpu as pltpu
from jax.sharding import PartitionSpec as P

MESH = pl.DeviceIdType.MESH
BF16, F32 = jnp.bfloat16, jnp.float32
GELU_C = math.sqrt(2.0 / math.pi)

NZ, NYH, NX, NYL = 8, 4, 4, 2
NQ = NX * NYL
TOK = 16
BLK = NYH * TOK
CH = 2 * BLK
NCH = 4
TILE = 256
POS = {1: 0, 7: 1, 2: 2, 6: 3, 3: 4, 5: 5, 0: 6, 4: 7}
DIST = {p: d for d, p in POS.items()}
NEAR, FAR = (1, 7, 2, 6), (3, 5, 4)
YHOPS = [2, 1, 3]
HOPS = [(2, 1), (2, 0), (1, 1), (3, 1), (1, 0), (3, 0), (0, 1)]

ORDER = [
    ("start",), ("ring", 1, 0), ("take", 0, 3), ("take", 0, 1), ("take", 0, 2), ("ring", 1, 3),
    ("ring", 1, 1), ("ring", 1, 2), ("ring", 2, 0), ("weights",), ("mul", 0), ("ring", 2, 3),
    ("ring", 2, 1), ("scatter", 0), ("ring", 2, 2), ("mul", 1), ("ring", 3, 3), ("ring", 3, 0),
    ("scatter", 1), ("ring", 3, 1), ("ring", 3, 2), ("mul", 2), ("act", 0), ("take", 4, 0),
    ("scatter", 2), ("take", 4, 1), ("take", 4, 2), ("take", 4, 3), ("mul", 3), ("scatter", 3),
    ("act", 2), ("act", 1), ("share", 0), ("act", 3), ("back", 0), ("share", 2), ("back", 2),
    ("share", 1), ("share", 3), ("back", 1), ("back", 3), ("far", 3), ("far", 5), ("far", 4),
    ("near",), ("grads", 1), ("grads", 0), ("drain",), ("end",),
]


def activate(pre, hidden_grad):
    inner = GELU_C * (pre + 0.044715 * pre * pre * pre)
    t = jnp.tanh(inner)
    value = 0.5 * pre * (1.0 + t)
    slope = 0.5 * (1.0 + t) + 0.5 * pre * (1.0 - t * t) * GELU_C * (
        1.0 + 3.0 * 0.044715 * pre * pre
    )
    return value.astype(BF16), (slope * hidden_grad).astype(BF16)


def kernel(
    x_hbm, win_hbm, wout_hbm, og_hbm,
    gi_ref, gwin_hbm, gwout_hbm,
    act, win, wout, part, crecv, sendb, own32, rrecv, agall, hid, pg,
    g0, gsend, grecv, f0, fsend, frecv, tsend, trecv, y0, ysend, yrecv, gw,
    lsem, ssem, agsem, csem, rsem, zsem, fsem, tsem, ysem,
):
    row, col = lax.axis_index("row"), lax.axis_index("col")
    core = lax.rem(row, 2)
    x = lax.rem(lax.div(row, 2), NX)
    ylo = lax.div(row, 2 * NX)
    yhi, z = lax.div(col, NZ), lax.rem(col, NZ)
    q = ylo * NX + x
    ncol = win.shape[1]
    half = ncol // NYL

    def at(dx=0, dy=0, dc=0, e=0, d=0):
        r = lax.rem(ylo + dy, NYL) * (2 * NX) + lax.rem(x + dx, NX) * 2 + lax.rem(core + dc, 2)
        c = lax.rem(yhi + e, NYH) * NZ + lax.rem(z + d, NZ)
        return (r, c)

    def chip(dx, dy):
        return lax.rem(ylo + dy, NYL) * NX + lax.rem(x + dx, NX)

    own = pl.ds(POS[0] * BLK, TOK)
    loads = [
        pltpu.make_async_copy(x_hbm, act.at[0, own], lsem.at[0]),
        pltpu.make_async_copy(og_hbm, act.at[1, own], lsem.at[1]),
        pltpu.make_async_copy(win_hbm, win, lsem.at[2]),
        pltpu.make_async_copy(wout_hbm, wout, lsem.at[3]),
    ]
    for c in loads:
        c.start()
    peers = (
        [at(dc=1)]
        + [at(dx=dx, dy=dy) for dx, dy in HOPS]
        + [at(e=e) for e in range(1, NYH)]
        + [at(d=d) for d in range(1, NZ)]
    )
    barrier = pltpu.get_barrier_semaphore()
    for p in peers:
        pl.semaphore_signal(barrier, inc=1, device_id=p, device_id_type=MESH)
    pl.semaphore_wait(barrier, len(peers))
    loads[0].wait()
    loads[1].wait()

    sent = []

    def send(src, dst, recv_sem, device):
        c = pltpu.make_async_remote_copy(
            src_ref=src, dst_ref=dst, send_sem=ssem.at[len(sent)], recv_sem=recv_sem,
            device_id=device, device_id_type=MESH,
        )
        c.start()
        sent.append(c)

    def arrived(ref, sem):
        pltpu.make_async_copy(ref, ref, sem).wait()

    def piece(d, e):
        return act.at[:, pl.ds(POS[d] * BLK + e * TOK, TOK)]

    def half_piece(a, d, e):
        return act.at[a, pl.ds(POS[d] * BLK + e * TOK, TOK)]

    down, up = at(d=NZ - 1), at(d=1)

    def forward(d, e):
        if d < 3:
            send(piece(d, e), piece(d + 1, e), agsem.at[POS[d + 1], e], down)
        if d == 3:
            send(half_piece(0, 3, e), half_piece(0, 4, e), agsem.at[POS[4], e], down)
        if d == 0 or d > 5:
            to = (d - 1) % NZ
            send(piece(d, e), piece(to, e), agsem.at[POS[to], e], up)
        if d == 5:
            send(half_piece(1, 5, e), half_piece(1, 4, e), agsem.at[NZ, e], up)

    def take(d, e):
        if d == 4:
            arrived(half_piece(0, 4, e), agsem.at[POS[4], e])
            arrived(half_piece(1, 4, e), agsem.at[NZ, e])
        else:
            arrived(piece(d, e), agsem.at[POS[d], e])
            forward(d, e)

    def take_ring(i, e):
        take(i, e)
        take(NZ - i, e)

    def multiply(ci):
        rows = pl.ds(ci * CH, CH)
        pre = jnp.dot(act[0, rows], win[...], preferred_element_type=F32)
        part[ci, 0, 0] = pre[:BLK]
        part[ci, 1, 0] = pre[BLK:]
        hg = lax.dot_general(
            act[1, rows], wout[...], (((1,), (1,)), ((), ())), preferred_element_type=F32
        )
        part[ci, 0, 1] = hg[:BLK]
        part[ci, 1, 1] = hg[BLK:]
        send(part.at[ci, 1 - core], crecv.at[ci], csem.at[0, ci], at(dc=1))

    def scatter(ci):
        arrived(crecv.at[ci], csem.at[0, ci])
        for k in range(NQ):
            r, c = pl.ds((k % NX) * TOK, TOK), pl.ds((k // NX) * half, half)
            total = part[ci, core, :, r, c] + crecv[ci, :, r, c]
            own32[ci, k] = total
            sendb[ci, k] = total.astype(BF16)
        for k, (dx, dy) in enumerate(HOPS):
            send(sendb.at[ci, chip(dx, dy)], rrecv.at[ci, k], rsem.at[0, ci], at(dx=dx, dy=dy))

    def activation(ci):
        arrived(rrecv.at[ci], rsem.at[0, ci])
        total = own32[ci, q]
        for k in range(NQ - 1):
            total = total + rrecv[ci, k].astype(F32)
        value, slope = activate(total[0], total[1])
        agall[ci, core, q, 0] = value
        agall[ci, core, q, 1] = slope
        for dx, dy in HOPS:
            send(agall.at[ci, core, q], agall.at[ci, core, q], rsem.at[1, ci], at(dx=dx, dy=dy))

    def share(ci):
        arrived(rrecv.at[ci], rsem.at[1, ci])
        send(agall.at[ci, core], agall.at[ci, core], csem.at[1, ci], at(dc=1))

    def back(ci):
        arrived(agall.at[ci, 0], csem.at[1, ci])
        for h in range(2):
            for k in range(NQ):
                r = pl.ds(ci * CH + h * BLK + (k % NX) * TOK, TOK)
                c = pl.ds((k // NX) * half, half)
                hid[r, c] = agall[ci, h, k, 0]
                pg[r, c] = agall[ci, h, k, 1]
        g = lax.dot_general(
            pg[pl.ds(ci * CH, CH)], win[...], (((1,), (1,)), ((), ())), preferred_element_type=F32
        )
        for h in range(2):
            d = DIST[2 * ci + h]
            block = g[h * BLK:(h + 1) * BLK]
            if d == 0:
                g0[...] = block
            elif d in NEAR:
                i = NEAR.index(d)
                gsend[i] = block.astype(BF16)
                send(gsend.at[i], grecv.at[i], zsem.at[i], at(d=d))
            else:
                i = FAR.index(d)
                f0[i] = block[:TOK]
                fsend[i] = block[TOK:].astype(BF16).reshape(fsend.shape[1:])
                for e in YHOPS:
                    send(fsend.at[i, e - 1], frecv.at[i, e - 1], fsem.at[i], at(e=e))

    def far(d):
        i = FAR.index(d)
        arrived(frecv.at[i], fsem.at[i])
        total = f0[i]
        for e in range(NYH - 1):
            total = total + frecv[i, e].astype(F32)
        tsend[i] = total.astype(BF16)
        send(tsend.at[i], trecv.at[i], tsem.at[i], at(d=d))

    def weight_grads(a):
        lhs, rhs, dst = ((hid, act.at[1], gwout_hbm), (act.at[0], pg, gwin_hbm))[a]
        for i in range(lhs.shape[1] // TILE):
            r = pl.ds(i * TILE, TILE)
            gw[a, r] = lax.dot_general(
                lhs[:, r], rhs[...], (((0,), (0,)), ((), ())), preferred_element_type=F32
            ).astype(BF16)
            c = pltpu.make_async_copy(gw.at[a, r], dst.at[r], lsem.at[4 + a * 3 + i])
            c.start()
            stores.append(c)

    def gather_start():
        forward(0, 0)
        for e in YHOPS:
            send(piece(0, 0), piece(0, e), agsem.at[POS[0], e], at(e=NYH - e))

    def weights_ready():
        loads[2].wait()
        loads[3].wait()

    stores = []

    def near():
        total = g0[...]
        for i in range(len(NEAR)):
            arrived(grecv.at[i], zsem.at[i])
            total = total + grecv[i].astype(F32)
        y0[...] = total[:TOK]
        ysend[...] = total[TOK:].astype(BF16).reshape(ysend.shape)
        for e in YHOPS:
            send(ysend.at[e - 1], yrecv.at[e - 1], ysem.at[0], at(e=e))

    def finish():
        total = y0[...]
        arrived(yrecv, ysem.at[0])
        for e in range(NYH - 1):
            total = total + yrecv[e].astype(F32)
        for i in range(len(FAR)):
            arrived(trecv.at[i], tsem.at[i])
            total = total + trecv[i].astype(F32)
        gi_ref[...] = total.astype(BF16)

    def drain():
        for c in sent:
            c.wait_send()
        for c in stores:
            c.wait()

    steps = {
        "start": gather_start, "take": take, "ring": take_ring, "weights": weights_ready,
        "mul": multiply, "scatter": scatter, "act": activation, "share": share, "back": back,
        "far": far, "grads": weight_grads, "near": near, "drain": drain, "end": finish,
    }
    for name, *args in ORDER:
        steps[name](*args)


N_SENDS = 32 + 3 + 2 * NCH + 2 * 7 * NCH + len(NEAR) + 4 * len(FAR) + (NYH - 1)


def store(*refs):
    n = len(refs) // 2
    copies = [
        pltpu.make_async_copy(src, dst, refs[-1].at[i])
        for i, (src, dst) in enumerate(zip(refs[:n], refs[n:2 * n]))
    ]
    for c in copies:
        c.start()
    for c in copies:
        c.wait()


def local(inputs, w_in, w_out, out_grad):
    feat, ff = w_in.shape
    half = ff // NYL
    tokens = TOK * NYH * NZ
    any_spec = pl.BlockSpec(memory_space=pl.ANY)
    vmem = pltpu.VMEM
    out_shape = tuple(jax.ShapeDtypeStruct(a.shape, BF16) for a in (inputs, w_in, w_out))
    outs = pl.pallas_call(
        kernel,
        out_shape=out_shape,
        in_specs=[any_spec] * 4,
        out_specs=(pl.BlockSpec(memory_space=pltpu.VMEM), any_spec, any_spec),
        scratch_shapes=[
            vmem((2, tokens, feat), BF16),
            vmem((feat, ff), BF16),
            vmem((ff, feat), BF16),
            vmem((NCH, 2, 2, BLK, ff), F32),
            vmem((NCH, 2, BLK, ff), F32),
            vmem((NCH, NQ, 2, TOK, half), BF16),
            vmem((NCH, NQ, 2, TOK, half), F32),
            vmem((NCH, NQ - 1, 2, TOK, half), BF16),
            vmem((NCH, 2, NQ, 2, TOK, half), BF16),
            vmem((tokens, ff), BF16),
            vmem((tokens, ff), BF16),
            vmem((BLK, feat), F32),
            vmem((len(NEAR), BLK, feat), BF16),
            vmem((len(NEAR), BLK, feat), BF16),
            vmem((len(FAR), TOK, feat), F32),
            vmem((len(FAR), NYH - 1, TOK, feat), BF16),
            vmem((len(FAR), NYH - 1, TOK, feat), BF16),
            vmem((len(FAR), TOK, feat), BF16),
            vmem((len(FAR), TOK, feat), BF16),
            vmem((TOK, feat), F32),
            vmem((NYH - 1, TOK, feat), BF16),
            vmem((NYH - 1, TOK, feat), BF16),
            vmem((2, feat, ff), BF16),
            pltpu.SemaphoreType.DMA((10,)),
            pltpu.SemaphoreType.DMA((N_SENDS,)),
            pltpu.SemaphoreType.DMA((NZ + 1, NYH)),
            pltpu.SemaphoreType.DMA((2, NCH)),
            pltpu.SemaphoreType.DMA((2, NCH)),
            pltpu.SemaphoreType.DMA((len(NEAR),)),
            pltpu.SemaphoreType.DMA((len(FAR),)),
            pltpu.SemaphoreType.DMA((len(FAR),)),
            pltpu.SemaphoreType.DMA((1,)),
        ],
        compiler_params=pltpu.CompilerParams(
            collective_id=0, has_side_effects=True, vmem_limit_bytes=48 * 2**20
        ),
        cost_estimate=pl.CostEstimate(
            flops=10 * tokens * feat * ff, bytes_accessed=8 * feat * ff, transcendentals=0
        ),
    )(*(pltpu.with_memory_space_constraint(a, pltpu.HBM) for a in (inputs, w_in, w_out, out_grad)))
    return pl.pallas_call(
        store,
        out_shape=out_shape,
        in_specs=[any_spec] * 3,
        out_specs=(any_spec,) * 3,
        scratch_shapes=[pltpu.SemaphoreType.DMA((3,))],
        compiler_params=pltpu.CompilerParams(vmem_limit_bytes=2**20),
        cost_estimate=pl.CostEstimate(flops=0, bytes_accessed=8 * feat * ff, transcendentals=0),
    )(*(pltpu.with_memory_space_constraint(a, pltpu.VMEM) for a in outs))


def solution(mesh):
    return jax.shard_map(
        local,
        mesh=mesh,
        in_specs=(P("col", "row"), P("row", "col"), P("col", "row"), P("col", "row")),
        out_specs=(P("col", "row"), P("row", "col"), P("col", "row")),
        check_vma=False,
    )
```

```python
import math

import jax
import jax.numpy as jnp
from jax import lax
from jax.experimental import pallas as pl
from jax.experimental.pallas import tpu as pltpu
from jax.sharding import PartitionSpec as P

MESH = pl.DeviceIdType.MESH
BF16, F32 = jnp.bfloat16, jnp.float32
GELU_C = math.sqrt(2.0 / math.pi)

NZ, NYH, NX, NYL = 8, 4, 4, 2
NQ = NX * NYL
TOK = 16
BLK = NYH * TOK
CH = 2 * BLK
NCH = 4
TILE = 256
POS = {1: 0, 7: 1, 2: 2, 6: 3, 3: 4, 5: 5, 0: 6, 4: 7}
DIST = {p: d for d, p in POS.items()}
NEAR, FAR = (1, 7, 2, 6), (3, 5, 4)
YHOPS = [2, 1, 3]
HOPS = [(2, 1), (2, 0), (1, 1), (3, 1), (1, 0), (3, 0), (0, 1)]

ORDER = [
    ("start",), ("ring", 1, 0), ("take", 0, 3), ("take", 0, 1), ("take", 0, 2), ("ring", 1, 3),
    ("ring", 1, 1), ("ring", 1, 2), ("ring", 2, 0), ("weights",), ("mul", 0), ("ring", 2, 3),
    ("ring", 2, 1), ("scatter", 0), ("ring", 2, 2), ("mul", 1), ("ring", 3, 3), ("ring", 3, 0),
    ("scatter", 1), ("ring", 3, 1), ("ring", 3, 2), ("mul", 2), ("act", 0), ("take", 4, 0),
    ("scatter", 2), ("take", 4, 1), ("take", 4, 2), ("take", 4, 3), ("mul", 3), ("scatter", 3),
    ("act", 2), ("act", 1), ("share", 0), ("act", 3), ("back", 0), ("share", 2), ("back", 2),
    ("share", 1), ("share", 3), ("back", 1), ("back", 3), ("far", 3), ("far", 5), ("far", 4),
    ("near",), ("grads", 1), ("grads", 0), ("drain",), ("end",),
]


def activate(pre, hidden_grad):
    inner = GELU_C * (pre + 0.044715 * pre * pre * pre)
    t = jnp.tanh(inner)
    value = 0.5 * pre * (1.0 + t)
    slope = 0.5 * (1.0 + t) + 0.5 * pre * (1.0 - t * t) * GELU_C * (
        1.0 + 3.0 * 0.044715 * pre * pre
    )
    return value.astype(BF16), (slope * hidden_grad).astype(BF16)


def kernel(
    x_hbm, win_hbm, wout_hbm, og_hbm,
    gi_ref, gwin_hbm, gwout_hbm,
    act, win, wout, part, crecv, sendb, own32, rrecv, agall, hid, pg,
    g0, gsend, grecv, f0, fsend, frecv, tsend, trecv, y0, ysend, yrecv, gw,
    lsem, ssem, agsem, csem, rsem, zsem, fsem, tsem, ysem,
):
    row, col = lax.axis_index("row"), lax.axis_index("col")
    core = lax.rem(row, 2)
    x = lax.rem(lax.div(row, 2), NX)
    ylo = lax.div(row, 2 * NX)
    yhi, z = lax.div(col, NZ), lax.rem(col, NZ)
    q = ylo * NX + x
    ncol = win.shape[1]
    half = ncol // NYL

    def at(dx=0, dy=0, dc=0, e=0, d=0):
        r = lax.rem(ylo + dy, NYL) * (2 * NX) + lax.rem(x + dx, NX) * 2 + lax.rem(core + dc, 2)
        c = lax.rem(yhi + e, NYH) * NZ + lax.rem(z + d, NZ)
        return (r, c)

    def chip(dx, dy):
        return lax.rem(ylo + dy, NYL) * NX + lax.rem(x + dx, NX)

    own = pl.ds(POS[0] * BLK, TOK)
    loads = [
        pltpu.make_async_copy(x_hbm, act.at[0, own], lsem.at[0]),
        pltpu.make_async_copy(og_hbm, act.at[1, own], lsem.at[1]),
        pltpu.make_async_copy(win_hbm, win, lsem.at[2]),
        pltpu.make_async_copy(wout_hbm, wout, lsem.at[3]),
    ]
    for c in loads:
        c.start()
    peers = (
        [at(dc=1)]
        + [at(dx=dx, dy=dy) for dx, dy in HOPS]
        + [at(e=e) for e in range(1, NYH)]
        + [at(d=d) for d in (1, NZ - 1)]
    )
    barrier = pltpu.get_barrier_semaphore()
    for p in peers:
        pl.semaphore_signal(barrier, inc=1, device_id=p, device_id_type=MESH)
    pl.semaphore_wait(barrier, len(peers))
    loads[0].wait()
    loads[1].wait()

    sent = []

    def send(src, dst, recv_sem, device):
        c = pltpu.make_async_remote_copy(
            src_ref=src, dst_ref=dst, send_sem=ssem.at[len(sent)], recv_sem=recv_sem,
            device_id=device, device_id_type=MESH,
        )
        c.start()
        sent.append(c)

    def arrived(ref, sem):
        pltpu.make_async_copy(ref, ref, sem).wait()

    def piece(d, e):
        return act.at[:, pl.ds(POS[d] * BLK + e * TOK, TOK)]

    def half_piece(a, d, e):
        return act.at[a, pl.ds(POS[d] * BLK + e * TOK, TOK)]

    down, up = at(d=NZ - 1), at(d=1)

    def forward(d, e):
        if d < 3:
            send(piece(d, e), piece(d + 1, e), agsem.at[POS[d + 1], e], down)
        if d == 3:
            send(half_piece(0, 3, e), half_piece(0, 4, e), agsem.at[POS[4], e], down)
        if d == 0 or d > 5:
            to = (d - 1) % NZ
            send(piece(d, e), piece(to, e), agsem.at[POS[to], e], up)
        if d == 5:
            send(half_piece(1, 5, e), half_piece(1, 4, e), agsem.at[NZ, e], up)

    def take(d, e):
        if d == 4:
            arrived(half_piece(0, 4, e), agsem.at[POS[4], e])
            arrived(half_piece(1, 4, e), agsem.at[NZ, e])
        else:
            arrived(piece(d, e), agsem.at[POS[d], e])
            forward(d, e)

    def take_ring(i, e):
        take(i, e)
        take(NZ - i, e)

    def multiply(ci):
        rows = pl.ds(ci * CH, CH)
        pre = jnp.dot(act[0, rows], win[...], preferred_element_type=F32)
        part[ci, 0, 0] = pre[:BLK]
        part[ci, 1, 0] = pre[BLK:]
        hg = lax.dot_general(
            act[1, rows], wout[...], (((1,), (1,)), ((), ())), preferred_element_type=F32
        )
        part[ci, 0, 1] = hg[:BLK]
        part[ci, 1, 1] = hg[BLK:]
        send(part.at[ci, 1 - core], crecv.at[ci], csem.at[0, ci], at(dc=1))

    def scatter(ci):
        arrived(crecv.at[ci], csem.at[0, ci])
        for k in range(NQ):
            r, c = pl.ds((k % NX) * TOK, TOK), pl.ds((k // NX) * half, half)
            total = part[ci, core, :, r, c] + crecv[ci, :, r, c]
            own32[ci, k] = total
            sendb[ci, k] = total.astype(BF16)
        for k, (dx, dy) in enumerate(HOPS):
            send(sendb.at[ci, chip(dx, dy)], rrecv.at[ci, k], rsem.at[0, ci], at(dx=dx, dy=dy))

    def activation(ci):
        arrived(rrecv.at[ci], rsem.at[0, ci])
        total = own32[ci, q]
        for k in range(NQ - 1):
            total = total + rrecv[ci, k].astype(F32)
        value, slope = activate(total[0], total[1])
        agall[ci, core, q, 0] = value
        agall[ci, core, q, 1] = slope
        for dx, dy in HOPS:
            send(agall.at[ci, core, q], agall.at[ci, core, q], rsem.at[1, ci], at(dx=dx, dy=dy))

    def share(ci):
        arrived(rrecv.at[ci], rsem.at[1, ci])
        send(agall.at[ci, core], agall.at[ci, core], csem.at[1, ci], at(dc=1))

    def back(ci):
        arrived(agall.at[ci, 0], csem.at[1, ci])
        for h in range(2):
            for k in range(NQ):
                r = pl.ds(ci * CH + h * BLK + (k % NX) * TOK, TOK)
                c = pl.ds((k // NX) * half, half)
                hid[r, c] = agall[ci, h, k, 0]
                pg[r, c] = agall[ci, h, k, 1]
        g = lax.dot_general(
            pg[pl.ds(ci * CH, CH)], win[...], (((1,), (1,)), ((), ())), preferred_element_type=F32
        )
        for h in range(2):
            d = DIST[2 * ci + h]
            block = g[h * BLK:(h + 1) * BLK]
            if d == 0:
                g0[...] = block
            elif d in NEAR:
                i = NEAR.index(d)
                gsend[i] = block.astype(BF16)
                send(gsend.at[i], grecv.at[i], zsem.at[i], at(d=d))
            else:
                i = FAR.index(d)
                f0[i] = block[:TOK]
                fsend[i] = block[TOK:].astype(BF16).reshape(fsend.shape[1:])
                for e in YHOPS:
                    send(fsend.at[i, e - 1], frecv.at[i, e - 1], fsem.at[i], at(e=e))

    def far(d):
        i = FAR.index(d)
        arrived(frecv.at[i], fsem.at[i])
        total = f0[i]
        for e in range(NYH - 1):
            total = total + frecv[i, e].astype(F32)
        tsend[i] = total.astype(BF16)
        send(tsend.at[i], trecv.at[i], tsem.at[i], at(d=d))

    def weight_grads(a):
        lhs, rhs, dst = ((hid, act.at[1], gwout_hbm), (act.at[0], pg, gwin_hbm))[a]
        for i in range(lhs.shape[1] // TILE):
            r = pl.ds(i * TILE, TILE)
            gw[a, r] = lax.dot_general(
                lhs[:, r], rhs[...], (((0,), (0,)), ((), ())), preferred_element_type=F32
            ).astype(BF16)
            c = pltpu.make_async_copy(gw.at[a, r], dst.at[r], lsem.at[4 + a * 3 + i])
            c.start()
            stores.append(c)

    def gather_start():
        forward(0, 0)
        for e in YHOPS:
            send(piece(0, 0), piece(0, e), agsem.at[POS[0], e], at(e=NYH - e))

    def weights_ready():
        loads[2].wait()
        loads[3].wait()

    stores = []

    def near():
        total = g0[...]
        for i in range(len(NEAR)):
            arrived(grecv.at[i], zsem.at[i])
            total = total + grecv[i].astype(F32)
        y0[...] = total[:TOK]
        ysend[...] = total[TOK:].astype(BF16).reshape(ysend.shape)
        for e in YHOPS:
            send(ysend.at[e - 1], yrecv.at[e - 1], ysem.at[0], at(e=e))

    def finish():
        total = y0[...]
        arrived(yrecv, ysem.at[0])
        for e in range(NYH - 1):
            total = total + yrecv[e].astype(F32)
        for i in range(len(FAR)):
            arrived(trecv.at[i], tsem.at[i])
            total = total + trecv[i].astype(F32)
        gi_ref[...] = total.astype(BF16)

    def drain():
        for c in sent:
            c.wait_send()
        for c in stores:
            c.wait()

    steps = {
        "start": gather_start, "take": take, "ring": take_ring, "weights": weights_ready,
        "mul": multiply, "scatter": scatter, "act": activation, "share": share, "back": back,
        "far": far, "grads": weight_grads, "near": near, "drain": drain, "end": finish,
    }
    for name, *args in ORDER:
        steps[name](*args)


N_SENDS = 32 + 3 + 2 * NCH + 2 * 7 * NCH + len(NEAR) + 4 * len(FAR) + (NYH - 1)


def store(*refs):
    n = len(refs) // 2
    copies = [
        pltpu.make_async_copy(src, dst, refs[-1].at[i])
        for i, (src, dst) in enumerate(zip(refs[:n], refs[n:2 * n]))
    ]
    for c in copies:
        c.start()
    for c in copies:
        c.wait()


def local(inputs, w_in, w_out, out_grad):
    feat, ff = w_in.shape
    half = ff // NYL
    tokens = TOK * NYH * NZ
    any_spec = pl.BlockSpec(memory_space=pl.ANY)
    vmem = pltpu.VMEM
    out_shape = tuple(jax.ShapeDtypeStruct(a.shape, BF16) for a in (inputs, w_in, w_out))
    outs = pl.pallas_call(
        kernel,
        out_shape=out_shape,
        in_specs=[any_spec] * 4,
        out_specs=(pl.BlockSpec(memory_space=pltpu.VMEM), any_spec, any_spec),
        scratch_shapes=[
            vmem((2, tokens, feat), BF16),
            vmem((feat, ff), BF16),
            vmem((ff, feat), BF16),
            vmem((NCH, 2, 2, BLK, ff), F32),
            vmem((NCH, 2, BLK, ff), F32),
            vmem((NCH, NQ, 2, TOK, half), BF16),
            vmem((NCH, NQ, 2, TOK, half), F32),
            vmem((NCH, NQ - 1, 2, TOK, half), BF16),
            vmem((NCH, 2, NQ, 2, TOK, half), BF16),
            vmem((tokens, ff), BF16),
            vmem((tokens, ff), BF16),
            vmem((BLK, feat), F32),
            vmem((len(NEAR), BLK, feat), BF16),
            vmem((len(NEAR), BLK, feat), BF16),
            vmem((len(FAR), TOK, feat), F32),
            vmem((len(FAR), NYH - 1, TOK, feat), BF16),
            vmem((len(FAR), NYH - 1, TOK, feat), BF16),
            vmem((len(FAR), TOK, feat), BF16),
            vmem((len(FAR), TOK, feat), BF16),
            vmem((TOK, feat), F32),
            vmem((NYH - 1, TOK, feat), BF16),
            vmem((NYH - 1, TOK, feat), BF16),
            vmem((2, feat, ff), BF16),
            pltpu.SemaphoreType.DMA((10,)),
            pltpu.SemaphoreType.DMA((N_SENDS,)),
            pltpu.SemaphoreType.DMA((NZ + 1, NYH)),
            pltpu.SemaphoreType.DMA((2, NCH)),
            pltpu.SemaphoreType.DMA((2, NCH)),
            pltpu.SemaphoreType.DMA((len(NEAR),)),
            pltpu.SemaphoreType.DMA((len(FAR),)),
            pltpu.SemaphoreType.DMA((len(FAR),)),
            pltpu.SemaphoreType.DMA((1,)),
        ],
        compiler_params=pltpu.CompilerParams(
            collective_id=0, has_side_effects=True, vmem_limit_bytes=48 * 2**20
        ),
        cost_estimate=pl.CostEstimate(
            flops=10 * tokens * feat * ff, bytes_accessed=8 * feat * ff, transcendentals=0
        ),
    )(*(pltpu.with_memory_space_constraint(a, pltpu.HBM) for a in (inputs, w_in, w_out, out_grad)))
    return pl.pallas_call(
        store,
        out_shape=out_shape,
        in_specs=[any_spec] * 3,
        out_specs=(any_spec,) * 3,
        scratch_shapes=[pltpu.SemaphoreType.DMA((3,))],
        compiler_params=pltpu.CompilerParams(vmem_limit_bytes=2**20),
        cost_estimate=pl.CostEstimate(flops=0, bytes_accessed=8 * feat * ff, transcendentals=0),
    )(*(pltpu.with_memory_space_constraint(a, pltpu.VMEM) for a in outs))


def solution(mesh):
    return jax.shard_map(
        local,
        mesh=mesh,
        in_specs=(P("col", "row"), P("row", "col"), P("col", "row"), P("col", "row")),
        out_specs=(P("col", "row"), P("row", "col"), P("col", "row")),
        check_vma=False,
    )
```

```python
import math

import jax
import jax.numpy as jnp
from jax import lax
from jax.experimental import pallas as pl
from jax.experimental.pallas import tpu as pltpu
from jax.sharding import PartitionSpec as P

MESH = pl.DeviceIdType.MESH
BF16, F32 = jnp.bfloat16, jnp.float32
GELU_C = math.sqrt(2.0 / math.pi)

NZ, NYH, NX, NYL = 8, 4, 4, 2
NQ = NX * NYL
TOK = 16
BLK = NYH * TOK
CH = 2 * BLK
NCH = 4
TILE = 256
POS = {1: 0, 7: 1, 2: 2, 6: 3, 3: 4, 5: 5, 0: 6, 4: 7}
DIST = {p: d for d, p in POS.items()}
NEAR, FAR = (1, 7, 2, 6), (3, 5, 4)
YHOPS = [2, 1, 3]
HOPS = [(2, 1), (2, 0), (1, 1), (3, 1), (1, 0), (3, 0), (0, 1)]

ORDER = [
    ("start",), ("weights",), ("ring", 1, 0), ("take", 0, 3), ("take", 0, 1), ("take", 0, 2), ("ring", 1, 3),
    ("ring", 1, 1), ("ring", 1, 2), ("ring", 2, 0), ("mul", 0), ("ring", 2, 3),
    ("ring", 2, 1), ("scatter", 0), ("ring", 2, 2), ("mul", 1), ("ring", 3, 3), ("ring", 3, 0),
    ("scatter", 1), ("ring", 3, 1), ("ring", 3, 2), ("mul", 2), ("act", 0), ("take", 4, 0),
    ("scatter", 2), ("take", 4, 1), ("take", 4, 2), ("take", 4, 3), ("mul", 3), ("scatter", 3),
    ("act", 2), ("act", 1), ("share", 0), ("act", 3), ("back", 0), ("share", 2), ("back", 2),
    ("share", 1), ("share", 3), ("back", 1), ("back", 3), ("far", 3), ("far", 5), ("far", 4),
    ("near",), ("grads", 1), ("grads", 0), ("drain",), ("end",),
]


def activate(pre, hidden_grad):
    inner = GELU_C * (pre + 0.044715 * pre * pre * pre)
    t = jnp.tanh(inner)
    value = 0.5 * pre * (1.0 + t)
    slope = 0.5 * (1.0 + t) + 0.5 * pre * (1.0 - t * t) * GELU_C * (
        1.0 + 3.0 * 0.044715 * pre * pre
    )
    return value.astype(BF16), (slope * hidden_grad).astype(BF16)


def kernel(
    x_hbm, win_hbm, wout_hbm, og_hbm,
    gi_ref, gwin_hbm, gwout_hbm,
    act, win, wout, win_t, wout_t, part, crecv, sendb, own32, rrecv, agall, hid, pg,
    g0, gsend, grecv, f0, fsend, frecv, tsend, trecv, y0, ysend, yrecv, gw,
    lsem, ssem, agsem, csem, rsem, zsem, fsem, tsem, ysem,
):
    row, col = lax.axis_index("row"), lax.axis_index("col")
    core = lax.rem(row, 2)
    x = lax.rem(lax.div(row, 2), NX)
    ylo = lax.div(row, 2 * NX)
    yhi, z = lax.div(col, NZ), lax.rem(col, NZ)
    q = ylo * NX + x
    ncol = win.shape[1]
    half = ncol // NYL

    def at(dx=0, dy=0, dc=0, e=0, d=0):
        r = lax.rem(ylo + dy, NYL) * (2 * NX) + lax.rem(x + dx, NX) * 2 + lax.rem(core + dc, 2)
        c = lax.rem(yhi + e, NYH) * NZ + lax.rem(z + d, NZ)
        return (r, c)

    def chip(dx, dy):
        return lax.rem(ylo + dy, NYL) * NX + lax.rem(x + dx, NX)

    own = pl.ds(POS[0] * BLK, TOK)
    loads = [
        pltpu.make_async_copy(x_hbm, act.at[0, own], lsem.at[0]),
        pltpu.make_async_copy(og_hbm, act.at[1, own], lsem.at[1]),
        pltpu.make_async_copy(win_hbm, win, lsem.at[2]),
        pltpu.make_async_copy(wout_hbm, wout, lsem.at[3]),
    ]
    for c in loads:
        c.start()
    peers = (
        [at(dc=1)]
        + [at(dx=dx, dy=dy) for dx, dy in HOPS]
        + [at(e=e) for e in range(1, NYH)]
        + [at(d=d) for d in range(1, NZ)]
    )
    barrier = pltpu.get_barrier_semaphore()
    for p in peers:
        pl.semaphore_signal(barrier, inc=1, device_id=p, device_id_type=MESH)
    pl.semaphore_wait(barrier, len(peers))
    loads[0].wait()
    loads[1].wait()

    sent = []

    def send(src, dst, recv_sem, device):
        c = pltpu.make_async_remote_copy(
            src_ref=src, dst_ref=dst, send_sem=ssem.at[len(sent)], recv_sem=recv_sem,
            device_id=device, device_id_type=MESH,
        )
        c.start()
        sent.append(c)

    def arrived(ref, sem):
        pltpu.make_async_copy(ref, ref, sem).wait()

    def piece(d, e):
        return act.at[:, pl.ds(POS[d] * BLK + e * TOK, TOK)]

    def half_piece(a, d, e):
        return act.at[a, pl.ds(POS[d] * BLK + e * TOK, TOK)]

    down, up = at(d=NZ - 1), at(d=1)

    def forward(d, e):
        if d < 3:
            send(piece(d, e), piece(d + 1, e), agsem.at[POS[d + 1], e], down)
        if d == 3:
            send(half_piece(0, 3, e), half_piece(0, 4, e), agsem.at[POS[4], e], down)
        if d == 0 or d > 5:
            to = (d - 1) % NZ
            send(piece(d, e), piece(to, e), agsem.at[POS[to], e], up)
        if d == 5:
            send(half_piece(1, 5, e), half_piece(1, 4, e), agsem.at[NZ, e], up)

    def take(d, e):
        if d == 4:
            arrived(half_piece(0, 4, e), agsem.at[POS[4], e])
            arrived(half_piece(1, 4, e), agsem.at[NZ, e])
        else:
            arrived(piece(d, e), agsem.at[POS[d], e])
            forward(d, e)

    def take_ring(i, e):
        take(i, e)
        take(NZ - i, e)

    def multiply(ci):
        rows = pl.ds(ci * CH, CH)
        pre = jnp.dot(act[0, rows], win[...], preferred_element_type=F32)
        part[ci, 0, 0] = pre[:BLK]
        part[ci, 1, 0] = pre[BLK:]
        hg = jnp.dot(act[1, rows], wout_t[...], preferred_element_type=F32)
        part[ci, 0, 1] = hg[:BLK]
        part[ci, 1, 1] = hg[BLK:]
        send(part.at[ci, 1 - core], crecv.at[ci], csem.at[0, ci], at(dc=1))

    def scatter(ci):
        arrived(crecv.at[ci], csem.at[0, ci])
        for k in range(NQ):
            r, c = pl.ds((k % NX) * TOK, TOK), pl.ds((k // NX) * half, half)
            total = part[ci, core, :, r, c] + crecv[ci, :, r, c]
            own32[ci, k] = total
            sendb[ci, k] = total.astype(BF16)
        for k, (dx, dy) in enumerate(HOPS):
            send(sendb.at[ci, chip(dx, dy)], rrecv.at[ci, k], rsem.at[0, ci], at(dx=dx, dy=dy))

    def activation(ci):
        arrived(rrecv.at[ci], rsem.at[0, ci])
        total = own32[ci, q]
        for k in range(NQ - 1):
            total = total + rrecv[ci, k].astype(F32)
        value, slope = activate(total[0], total[1])
        agall[ci, core, q, 0] = value
        agall[ci, core, q, 1] = slope
        for dx, dy in HOPS:
            send(agall.at[ci, core, q], agall.at[ci, core, q], rsem.at[1, ci], at(dx=dx, dy=dy))

    def share(ci):
        arrived(rrecv.at[ci], rsem.at[1, ci])
        send(agall.at[ci, core], agall.at[ci, core], csem.at[1, ci], at(dc=1))

    def back(ci):
        arrived(agall.at[ci, 0], csem.at[1, ci])
        for h in range(2):
            for k in range(NQ):
                r = pl.ds(ci * CH + h * BLK + (k % NX) * TOK, TOK)
                c = pl.ds((k // NX) * half, half)
                hid[r, c] = agall[ci, h, k, 0]
                pg[r, c] = agall[ci, h, k, 1]
        g = jnp.dot(pg[pl.ds(ci * CH, CH)], win_t[...], preferred_element_type=F32)
        for h in range(2):
            d = DIST[2 * ci + h]
            block = g[h * BLK:(h + 1) * BLK]
            if d == 0:
                g0[...] = block
            elif d in NEAR:
                i = NEAR.index(d)
                gsend[i] = block.astype(BF16)
                send(gsend.at[i], grecv.at[i], zsem.at[i], at(d=d))
            else:
                i = FAR.index(d)
                f0[i] = block[:TOK]
                fsend[i] = block[TOK:].astype(BF16).reshape(fsend.shape[1:])
                for e in YHOPS:
                    send(fsend.at[i, e - 1], frecv.at[i, e - 1], fsem.at[i], at(e=e))

    def far(d):
        i = FAR.index(d)
        arrived(frecv.at[i], fsem.at[i])
        total = f0[i]
        for e in range(NYH - 1):
            total = total + frecv[i, e].astype(F32)
        tsend[i] = total.astype(BF16)
        send(tsend.at[i], trecv.at[i], tsem.at[i], at(d=d))

    def weight_grads(a):
        lhs, rhs, dst = ((hid, act.at[1], gwout_hbm), (act.at[0], pg, gwin_hbm))[a]
        for i in range(lhs.shape[1] // TILE):
            r = pl.ds(i * TILE, TILE)
            gw[a, r] = lax.dot_general(
                lhs[:, r], rhs[...], (((0,), (0,)), ((), ())), preferred_element_type=F32
            ).astype(BF16)
            c = pltpu.make_async_copy(gw.at[a, r], dst.at[r], lsem.at[4 + a * 3 + i])
            c.start()
            stores.append(c)

    def gather_start():
        forward(0, 0)
        for e in YHOPS:
            send(piece(0, 0), piece(0, e), agsem.at[POS[0], e], at(e=NYH - e))

    def weights_ready():
        loads[2].wait()
        win_t[...] = win[...].T
        loads[3].wait()
        wout_t[...] = wout[...].T

    stores = []

    def near():
        total = g0[...]
        for i in range(len(NEAR)):
            arrived(grecv.at[i], zsem.at[i])
            total = total + grecv[i].astype(F32)
        y0[...] = total[:TOK]
        ysend[...] = total[TOK:].astype(BF16).reshape(ysend.shape)
        for e in YHOPS:
            send(ysend.at[e - 1], yrecv.at[e - 1], ysem.at[0], at(e=e))

    def finish():
        total = y0[...]
        arrived(yrecv, ysem.at[0])
        for e in range(NYH - 1):
            total = total + yrecv[e].astype(F32)
        for i in range(len(FAR)):
            arrived(trecv.at[i], tsem.at[i])
            total = total + trecv[i].astype(F32)
        gi_ref[...] = total.astype(BF16)

    def drain():
        for c in sent:
            c.wait_send()
        for c in stores:
            c.wait()

    steps = {
        "start": gather_start, "take": take, "ring": take_ring, "weights": weights_ready,
        "mul": multiply, "scatter": scatter, "act": activation, "share": share, "back": back,
        "far": far, "grads": weight_grads, "near": near, "drain": drain, "end": finish,
    }
    for name, *args in ORDER:
        steps[name](*args)


N_SENDS = 32 + 3 + 2 * NCH + 2 * 7 * NCH + len(NEAR) + 4 * len(FAR) + (NYH - 1)


def store(*refs):
    n = len(refs) // 2
    copies = [
        pltpu.make_async_copy(src, dst, refs[-1].at[i])
        for i, (src, dst) in enumerate(zip(refs[:n], refs[n:2 * n]))
    ]
    for c in copies:
        c.start()
    for c in copies:
        c.wait()


def local(inputs, w_in, w_out, out_grad):
    feat, ff = w_in.shape
    half = ff // NYL
    tokens = TOK * NYH * NZ
    any_spec = pl.BlockSpec(memory_space=pl.ANY)
    vmem = pltpu.VMEM
    out_shape = tuple(jax.ShapeDtypeStruct(a.shape, BF16) for a in (inputs, w_in, w_out))
    outs = pl.pallas_call(
        kernel,
        out_shape=out_shape,
        in_specs=[any_spec] * 4,
        out_specs=(pl.BlockSpec(memory_space=pltpu.VMEM), any_spec, any_spec),
        scratch_shapes=[
            vmem((2, tokens, feat), BF16),
            vmem((feat, ff), BF16),
            vmem((ff, feat), BF16),
            vmem((ff, feat), BF16),
            vmem((feat, ff), BF16),
            vmem((NCH, 2, 2, BLK, ff), F32),
            vmem((NCH, 2, BLK, ff), F32),
            vmem((NCH, NQ, 2, TOK, half), BF16),
            vmem((NCH, NQ, 2, TOK, half), F32),
            vmem((NCH, NQ - 1, 2, TOK, half), BF16),
            vmem((NCH, 2, NQ, 2, TOK, half), BF16),
            vmem((tokens, ff), BF16),
            vmem((tokens, ff), BF16),
            vmem((BLK, feat), F32),
            vmem((len(NEAR), BLK, feat), BF16),
            vmem((len(NEAR), BLK, feat), BF16),
            vmem((len(FAR), TOK, feat), F32),
            vmem((len(FAR), NYH - 1, TOK, feat), BF16),
            vmem((len(FAR), NYH - 1, TOK, feat), BF16),
            vmem((len(FAR), TOK, feat), BF16),
            vmem((len(FAR), TOK, feat), BF16),
            vmem((TOK, feat), F32),
            vmem((NYH - 1, TOK, feat), BF16),
            vmem((NYH - 1, TOK, feat), BF16),
            vmem((2, feat, ff), BF16),
            pltpu.SemaphoreType.DMA((10,)),
            pltpu.SemaphoreType.DMA((N_SENDS,)),
            pltpu.SemaphoreType.DMA((NZ + 1, NYH)),
            pltpu.SemaphoreType.DMA((2, NCH)),
            pltpu.SemaphoreType.DMA((2, NCH)),
            pltpu.SemaphoreType.DMA((len(NEAR),)),
            pltpu.SemaphoreType.DMA((len(FAR),)),
            pltpu.SemaphoreType.DMA((len(FAR),)),
            pltpu.SemaphoreType.DMA((1,)),
        ],
        compiler_params=pltpu.CompilerParams(
            collective_id=0, has_side_effects=True, vmem_limit_bytes=48 * 2**20
        ),
        cost_estimate=pl.CostEstimate(
            flops=10 * tokens * feat * ff, bytes_accessed=8 * feat * ff, transcendentals=0
        ),
    )(*(pltpu.with_memory_space_constraint(a, pltpu.HBM) for a in (inputs, w_in, w_out, out_grad)))
    return pl.pallas_call(
        store,
        out_shape=out_shape,
        in_specs=[any_spec] * 3,
        out_specs=(any_spec,) * 3,
        scratch_shapes=[pltpu.SemaphoreType.DMA((3,))],
        compiler_params=pltpu.CompilerParams(vmem_limit_bytes=2**20),
        cost_estimate=pl.CostEstimate(flops=0, bytes_accessed=8 * feat * ff, transcendentals=0),
    )(*(pltpu.with_memory_space_constraint(a, pltpu.VMEM) for a in outs))


def solution(mesh):
    return jax.shard_map(
        local,
        mesh=mesh,
        in_specs=(P("col", "row"), P("row", "col"), P("col", "row"), P("col", "row")),
        out_specs=(P("col", "row"), P("row", "col"), P("col", "row")),
        check_vma=False,
    )
```
